256 devices in a mesh: pb: 8 (over x, core), ka: 32 (over z, y).
Axes of the slice: x: 4, y: 4, z: 8, core: 2. Of those that a mesh axis runs over, the one named last changes fastest.
Arguments:
- queries: bfloat16 [2048, 8192], P('pb', 'ka'), may hold values from -80 to 80
- keys: bfloat16 [16384, 1024], P('ka', 'pb'), may hold values from -8 to 8
- values: bfloat16 [16384, 1024], P('ka', 'pb'), may hold values from -6 to 6
- offset: int32 [1], replicated, may hold values from 0 to 224
Outputs:
- attended: bfloat16 [2048, 8192], P('pb', 'ka')
The draws below stay inside these ranges and needn't reach their ends.
All inputs are finite; a program needn't handle non-finite values.
Results may differ from the reference program's by a relative error of at most 0.0056.
Values may be sent and summed in bfloat16 or wider, within the bound.
No kernel may reach another device: no remote copies, remote signals or barrier semaphores. Data moves between devices by JAX's collectives and lax.ppermute only.
A program may use at most 128 MiB of HBM per device.

```python
import jax
import jax.numpy as jnp
from jax import lax

QUERY_HEAD_COUNT = 64
KEY_VALUE_HEADS = 8
HEAD_SIZE = 128
BLOCK = 64
KEYS_PER_SHARD = 512
WINDOW_TOKENS = 2048
CACHED_KEYS = 16384
QBLOCKS = 32
KBLOCKS = 256
N_KA = 32


def draw_queries(key, part):
    key = jax.random.fold_in(key, 11)
    key_base = jax.random.fold_in(key, 0)
    base_offset = jnp.clip(jax.random.normal(key_base, (WINDOW_TOKENS, QUERY_HEAD_COUNT * HEAD_SIZE), jnp.float32), -6.0, 6.0)
    return base_offset.astype(jnp.bfloat16)


def draw_keys(key, part):
    key = jax.random.fold_in(key, 23)
    base_offset = jnp.clip(jax.random.normal(key, (CACHED_KEYS, KEY_VALUE_HEADS * HEAD_SIZE), jnp.float32), -6.0, 6.0)
    return base_offset.astype(jnp.bfloat16)


def level_of(key, dims, cuts, low, top_value):
    level, own = 1.0, jax.random.fold_in(key, 6)
    for axis_at, shards_of in cuts:
        heights = jnp.exp(jax.random.uniform(jax.random.fold_in(own, axis_at), (shards_of,), jnp.float32, low / len(cuts), top_value / len(cuts)))
        level = level * jnp.repeat(heights, dims[axis_at] // shards_of).reshape([-1 if axis == axis_at else 1 for axis in range(len(dims))])
    return level


def gaussian(stream_key, dims, width, bound, cuts=(), held_as=jnp.bfloat16):
    gain = level_of(stream_key, dims, cuts, -0.22, 0.18) if cuts else 1.0
    drawn = jax.random.normal(stream_key, dims, jnp.float32) * width * gain
    return jnp.minimum(jnp.maximum(drawn, -bound), bound).astype(held_as)


def setup_inputs(seed: int = 0) -> dict:
    seeds = jax.random.split(jax.random.key(seed), 5)
    return {
        "queries": draw_queries(jax.random.fold_in(seeds[4], 71), 0),
        "keys": draw_keys(jax.random.fold_in(seeds[4], 71), 0),
        "values": gaussian(seeds[2], (CACHED_KEYS, KEY_VALUE_HEADS * HEAD_SIZE), 1.0, 6.0, ((0, 32), (1, 8))),
        "offset": jax.random.randint(seeds[3], (1,), 0, KBLOCKS - QBLOCKS + 1).astype(jnp.int32),
    }


NEGATIVE_LARGE = -1.0e30


def reference(queries, keys, values, offset):
    query_group = QUERY_HEAD_COUNT // KEY_VALUE_HEADS
    scale = HEAD_SIZE ** -0.5
    query_float = queries.astype(jnp.float32).reshape(WINDOW_TOKENS, KEY_VALUE_HEADS, query_group, HEAD_SIZE)
    qblock = (jnp.arange(WINDOW_TOKENS) // BLOCK).astype(jnp.int32)
    position = offset[0] + qblock

    def step(carry, rng):
        best, denom, accum = carry
        start_position = (rng * KEYS_PER_SHARD).astype(jnp.int32)
        key_rows_local = lax.dynamic_slice_in_dim(keys, start_position, KEYS_PER_SHARD, 0).astype(jnp.float32).reshape(KEYS_PER_SHARD, KEY_VALUE_HEADS, HEAD_SIZE)
        value_rows_local = lax.dynamic_slice_in_dim(values, start_position, KEYS_PER_SHARD, 0).astype(jnp.float32).reshape(KEYS_PER_SHARD, KEY_VALUE_HEADS, HEAD_SIZE)
        kblock = ((start_position + jnp.arange(KEYS_PER_SHARD)) // BLOCK).astype(jnp.int32)
        visible = kblock[None, :] <= position[:, None]
        mask = visible[:, None, None, :]
        scores = jnp.einsum("qgad,tgd->qgat", query_float, key_rows_local) * scale
        top = jnp.max(jnp.where(mask, scores, NEGATIVE_LARGE), axis=-1)
        expo = jnp.where(mask, jnp.exp(scores - top[..., None]), 0.0)
        total = jnp.sum(expo, axis=-1)
        rounded = lax.optimization_barrier(expo.astype(jnp.bfloat16)).astype(jnp.float32)
        mixed = jnp.einsum("qgat,tgd->qgad", rounded, value_rows_local)
        part = mixed / jnp.maximum(total, 1.0)[..., None]
        part = lax.optimization_barrier(part.astype(jnp.bfloat16)).astype(jnp.float32)
        newbest = jnp.maximum(best, top)
        keep = jnp.exp(best - newbest)
        scale_r = jnp.exp(top - newbest) * total
        accum = keep[..., None] * accum + scale_r[..., None] * part
        denom = keep * denom + scale_r
        return (newbest, denom, accum), None

    initial_carry = (jnp.full((WINDOW_TOKENS, KEY_VALUE_HEADS, query_group), NEGATIVE_LARGE, jnp.float32),
            jnp.zeros((WINDOW_TOKENS, KEY_VALUE_HEADS, query_group), jnp.float32),
            jnp.zeros((WINDOW_TOKENS, KEY_VALUE_HEADS, query_group, HEAD_SIZE), jnp.float32))
    (best, denom, accum), unused = lax.scan(step, initial_carry, jnp.arange(N_KA).astype(jnp.int32))
    return (accum / denom[..., None]).reshape(WINDOW_TOKENS, QUERY_HEAD_COUNT * HEAD_SIZE).astype(jnp.bfloat16)
```

```python
import functools
import math

import jax
import jax.numpy as jnp
from jax import lax
from jax.experimental import pallas as pl
from jax.experimental.pallas import tpu as pltpu
from jax.sharding import PartitionSpec as P

HEAD = 128
BLOCK = 64
CHUNK = 512
GROUPS = 8
ROWS = 256
STATS = 16
NEGATIVE_LARGE = -1e30
SCALE = HEAD ** (-0.5) * math.log2(math.e)
AXES = ("pb", "ka")


def device(x, c, z, y):
    return (x * 2 + c) * 32 + z * 4 + y


PLACES = [
    (x, c, z, y) for x in range(4) for c in range(2) for z in range(8) for y in range(4)
]


def moves(to):
    return [(device(*place), device(*to(*place))) for place in PLACES]


def shift(dx=0, dc=0, dy=0):
    return moves(lambda x, c, z, y: ((x + dx) % 4, (c + dc) % 2, z, (y + dy) % 4))


TO_HEAD = moves(lambda x, c, z, y: (z % 4, z // 4, 2 * x + c, y))


def send(array, pairs):
    return lax.ppermute(array, AXES, pairs)


def attend_kernel(info, *refs):
    q_refs, kv_hbm = refs[:4], refs[4:12]
    out_refs = refs[12:16]
    kv, vext, m_ref, acc, sems = refs[16:]
    copies = []
    for j in range(GROUPS):
        copy = pltpu.make_async_copy(kv_hbm[j], kv.at[info[j]], sems.at[j])
        copy.start()
        copies.append(copy)
    first = info[8]
    place = info[9]
    n_full = info[10]
    n_seen = info[11]
    for copy in copies:
        copy.wait()

    def extend(j, carry):
        vext[j, :, :HEAD] = kv[j, :, HEAD:]
        vext[j, :, HEAD:] = jnp.ones((CHUNK, HEAD), jnp.bfloat16)
        return carry

    lax.fori_loop(0, n_seen, extend, 0)
    select = (
        lax.broadcasted_iota(jnp.int32, (STATS, HEAD), 0)
        == lax.broadcasted_iota(jnp.int32, (STATS, HEAD), 1)
    ).astype(jnp.bfloat16)
    lane = lax.broadcasted_iota(jnp.int32, (ROWS, HEAD), 1)

    for i in range(4):
        m_ref[...] = jnp.full(m_ref.shape, NEGATIVE_LARGE, jnp.float32)
        acc[...] = jnp.zeros_like(acc)

        def step(j, masked, i=i):
            q = jnp.concatenate([q_refs[i][:, :HEAD], q_refs[i][:, HEAD:]], axis=0)
            s = lax.dot_general(
                q,
                kv[j, :, :HEAD],
                (((1,), (1,)), ((), ())),
                preferred_element_type=jnp.float32,
            )
            if masked:
                row = lax.broadcasted_iota(jnp.int32, s.shape, 0)
                col = lax.broadcasted_iota(jnp.int32, s.shape, 1)
                row_block = place + (row % ROWS) // BLOCK
                seen = first + j * 32 + col // BLOCK <= row_block
                s = jnp.where(seen, s, NEGATIVE_LARGE)
            m_old = m_ref[...]
            m_new = jnp.maximum(m_old, jnp.max(s, axis=1, keepdims=True))
            alpha = jnp.exp2((m_old - m_new) * SCALE)
            wide = jnp.concatenate([m_new] * (CHUNK // HEAD), axis=1)
            p = jnp.exp2((s - wide) * SCALE)
            if masked:
                p = jnp.where(seen, p, 0.0)
            m_ref[...] = m_new
            acc[...] = acc[...] * jnp.concatenate([alpha, alpha], axis=1) + jnp.dot(
                p.astype(jnp.bfloat16), vext[j], preferred_element_type=jnp.float32
            )

        lax.fori_loop(0, n_full, lambda j, carry: (step(j, False), carry)[1], 0)

        @pl.when(n_seen > n_full)
        def _():
            step(n_full, True)

        pieces = []
        for h in range(2):
            rows = pl.ds(h * ROWS, ROWS)
            total = acc[rows, HEAD:]
            out = acc[rows, :HEAD] / jnp.maximum(total, 1.0)
            out_refs[i][:ROWS, h * HEAD : (h + 1) * HEAD] = out.astype(jnp.bfloat16)
            for value, n in ((m_ref[rows, :], 3), (total, 2)):
                for _ in range(n):
                    piece = value.astype(jnp.bfloat16).astype(jnp.float32)
                    value = value - piece
                    pieces.append(piece)
        packed = jnp.zeros((ROWS, HEAD), jnp.float32)
        for n, piece in enumerate(pieces):
            packed = jnp.where(lane == n, piece, packed)
        stats = lax.dot_general(
            select,
            packed.astype(jnp.bfloat16),
            (((1,), (1,)), ((), ())),
            preferred_element_type=jnp.float32,
        )
        out_refs[i][ROWS:, :] = stats.astype(jnp.bfloat16)


def attend(info, qs, kvs):
    vmem = pl.BlockSpec(memory_space=pltpu.VMEM)
    return pl.pallas_call(
        attend_kernel,
        out_shape=[jax.ShapeDtypeStruct((ROWS + STATS, 2 * HEAD), jnp.bfloat16)] * 4,
        in_specs=[pl.BlockSpec(memory_space=pltpu.SMEM)]
        + [vmem] * 4
        + [pl.BlockSpec(memory_space=pl.ANY)] * 8,
        out_specs=[vmem] * 4,
        scratch_shapes=[
            pltpu.VMEM((GROUPS, CHUNK, 2 * HEAD), jnp.bfloat16),
            pltpu.VMEM((GROUPS, CHUNK, 2 * HEAD), jnp.bfloat16),
            pltpu.VMEM((2 * ROWS, HEAD), jnp.float32),
            pltpu.VMEM((2 * ROWS, 2 * HEAD), jnp.float32),
            pltpu.SemaphoreType.DMA((8,)),
        ],
        compiler_params=pltpu.CompilerParams(vmem_limit_bytes=32 << 20),
        name="attend",
    )(info, *qs, *kvs)


def combine_kernel(*refs):
    parts, out_ref = refs[:4], refs[4]
    stat = lax.broadcasted_iota(jnp.int32, (STATS, 2 * HEAD), 0)
    head = lax.broadcasted_iota(jnp.int32, (STATS, 2 * HEAD), 1) // HEAD
    is_top = (stat >= head * 5) & (stat < head * 5 + 3)
    is_total = (stat >= head * 5 + 3) & (stat < head * 5 + 5)

    def spread(ref, which):
        return lax.dot_general(
            ref[ROWS:, :],
            which.astype(jnp.bfloat16),
            (((0,), (0,)), ((), ())),
            preferred_element_type=jnp.float32,
        )

    tops = [spread(ref, is_top) for ref in parts]
    totals = [spread(ref, is_total) for ref in parts]
    best = functools.reduce(jnp.maximum, tops)
    weights = [jnp.exp2((t - best) * SCALE) * n for t, n in zip(tops, totals)]
    numer = sum(w * ref[:ROWS, :].astype(jnp.float32) for w, ref in zip(weights, parts))
    out_ref[...] = (numer / sum(weights)).astype(jnp.bfloat16)


def combine(parts):
    vmem = pl.BlockSpec(memory_space=pltpu.VMEM)
    return pl.pallas_call(
        combine_kernel,
        out_shape=jax.ShapeDtypeStruct((ROWS, 2 * HEAD), jnp.bfloat16),
        in_specs=[vmem] * 4,
        out_specs=vmem,
        name="combine",
    )(*parts)


def local(queries, keys, values, offset):
    pb, ka = lax.axis_index("pb"), lax.axis_index("ka")
    x, c, y = pb // 2, pb % 2, ka % 4
    around = (1, 3, 2)

    own = send(jnp.concatenate([keys, values], axis=1), TO_HEAD)
    qs = [queries] + [send(queries, shift(dy=d)) for d in around]
    near = [own] + [send(own, shift(dx=d)) for d in around]
    far = [send(a, shift(dc=1)) for a in near]

    slots = [(x - d) % 4 + 4 * c for d in (0,) + around]
    slots += [(x - d) % 4 + 4 * (1 - c) for d in (0,) + around]
    place = offset[0] + pb * (ROWS // BLOCK)
    first = 8 * y
    n_full = jnp.clip((place - first - 7) // 32 + 1, 0, GROUPS)
    n_seen = jnp.clip((place + 3 - first) // 32 + 1, 0, GROUPS)
    info = jnp.stack(slots + [first, place, n_full, n_seen]).astype(jnp.int32)
    parts = attend(info, qs, near + far)
    back = [parts[0]] + [
        send(part, shift(dy=-d)) for part, d in zip(parts[1:], around)
    ]
    return combine(back)


def solution(mesh):
    placed = (P("pb", "ka"), P("ka", "pb"), P("ka", "pb"), P())
    return jax.shard_map(
        local, mesh=mesh, in_specs=placed, out_specs=P("pb", "ka"), check_vma=False
    )
```

```python
import functools
import math

import jax
import jax.numpy as jnp
from jax import lax
from jax.experimental import pallas as pl
from jax.experimental.pallas import tpu as pltpu
from jax.sharding import PartitionSpec as P

HEAD = 128
BLOCK = 64
CHUNK = 512
GROUPS = 8
ROWS = 256
STATS = 16
NEGATIVE_LARGE = -1e30
UNSEEN = -1e29
SCALE = HEAD ** (-0.5) * math.log2(math.e)
AXES = ("pb", "ka")


def device(x, c, z, y):
    return (x * 2 + c) * 32 + z * 4 + y


PLACES = [
    (x, c, z, y) for x in range(4) for c in range(2) for z in range(8) for y in range(4)
]


def moves(to):
    return [(device(*place), device(*to(*place))) for place in PLACES]


def shift(dx=0, dc=0, dy=0):
    return moves(lambda x, c, z, y: ((x + dx) % 4, (c + dc) % 2, z, (y + dy) % 4))


TO_HEAD = moves(lambda x, c, z, y: (z % 4, z // 4, 2 * x + c, y))


def send(array, pairs):
    return lax.ppermute(array, AXES, pairs)


def attend_kernel(tiles, info, *refs):
    q_refs, refs = refs[:tiles], refs[tiles:]
    if tiles > 1:
        k_hbm, v_hbm, refs = refs[:GROUPS], refs[GROUPS : 2 * GROUPS], refs[2 * GROUPS :]
        out_refs, refs = refs[:tiles], refs[tiles:]
        keys, values, tops, totals, acc, sems = refs
        copies = []
        for j in range(GROUPS):
            for n, (hbm, buffer) in enumerate(((k_hbm, keys), (v_hbm, values))):
                copy = pltpu.make_async_copy(hbm[j], buffer.at[info[j]], sems.at[n, j])
                copy.start()
                copies.append(copy)
    else:
        keys, values, out_ref, tops, totals, acc = refs
        out_refs, copies = [out_ref], []
    first = info[8]
    place = info[9]
    n_full = info[10]
    n_seen = info[11]
    tops[...] = jnp.full(tops.shape, UNSEEN, jnp.float32)
    totals[...] = jnp.zeros_like(totals)
    acc[...] = jnp.zeros_like(acc)
    for copy in copies:
        copy.wait()

    def step(j, masked):
        key, value = keys[j], values[j]

        def scores(i):
            q = jnp.concatenate([q_refs[i][:, :HEAD], q_refs[i][:, HEAD:]], axis=0)
            s = lax.dot_general(
                q,
                key,
                (((1,), (1,)), ((), ())),
                preferred_element_type=jnp.float32,
            )
            if masked:
                row = lax.broadcasted_iota(jnp.int32, s.shape, 0)
                col = lax.broadcasted_iota(jnp.int32, s.shape, 1)
                seen = first + j * 32 + col // BLOCK <= place + (row % ROWS) // BLOCK
                s = jnp.where(seen, s, NEGATIVE_LARGE)
            return s

        def weights(i, s):
            rows = pl.ds(i * 2 * ROWS, 2 * ROWS)
            old = tops[rows, :]
            top = jnp.maximum(old, jnp.max(s, axis=1, keepdims=True))
            keep = jnp.exp2((old - top) * SCALE)
            p = jnp.exp2((s - jnp.concatenate([top] * 4, axis=1)) * SCALE)
            tops[rows, :] = top
            total = sum(p[:, n * HEAD : (n + 1) * HEAD] for n in range(4))
            totals[rows, :] = totals[rows, :] * keep + total
            return p.astype(jnp.bfloat16), keep

        def mix(i, p, keep):
            rows = pl.ds(i * 2 * ROWS, 2 * ROWS)
            mixed = jnp.dot(p, value, preferred_element_type=jnp.float32)
            acc[rows, :] = acc[rows, :] * keep + mixed

        s, before = scores(0), None
        for i in range(tiles):
            after = scores(i + 1) if i + 1 < tiles else None
            now = weights(i, s)
            if before is not None:
                mix(i - 1, *before)
            before, s = now, after
        mix(tiles - 1, *before)

    def full_step(j, carry):
        step(j, False)
        return carry

    lax.fori_loop(0, n_full, full_step, 0)

    @pl.when(n_seen > n_full)
    def _():
        step(n_full, True)

    lane = lax.broadcasted_iota(jnp.int32, (ROWS, HEAD), 1) % 4
    piece = lax.broadcasted_iota(jnp.int32, (STATS, ROWS), 0) // 4
    for i in range(tiles):
        stats = []
        for h in range(2):
            rows = pl.ds((2 * i + h) * ROWS, ROWS)
            total = jnp.sum(totals[rows, :], axis=1, keepdims=True)
            part = acc[rows, :] / jnp.maximum(total, 1.0)
            out_refs[i][:ROWS, h * HEAD : (h + 1) * HEAD] = part.astype(jnp.bfloat16)
            stats += [tops[rows, :], total]
        packed = jnp.where(
            lane < 2,
            jnp.where(lane == 0, stats[0], stats[1]),
            jnp.where(lane == 2, stats[2], stats[3]),
        )
        rest = packed.T[:STATS, :]
        high = rest.astype(jnp.bfloat16).astype(jnp.float32)
        rest = rest - high
        middle = rest.astype(jnp.bfloat16).astype(jnp.float32)
        low = jnp.where(piece == 2, rest - middle, 0.0)
        pieces = jnp.where(piece == 0, high, jnp.where(piece == 1, middle, low))
        out_refs[i][ROWS:, :] = pieces.astype(jnp.bfloat16)


VMEM = pl.BlockSpec(memory_space=pltpu.VMEM)
SMEM = pl.BlockSpec(memory_space=pltpu.SMEM)
ANY = pl.BlockSpec(memory_space=pl.ANY)
PART = jax.ShapeDtypeStruct((ROWS + STATS, 2 * HEAD), jnp.bfloat16)
SORTED = jax.ShapeDtypeStruct((GROUPS, CHUNK, HEAD), jnp.bfloat16)


def attend_others(info, qs, ks, vs):
    return pl.pallas_call(
        functools.partial(attend_kernel, 3),
        out_shape=[PART] * 3 + [SORTED] * 2,
        in_specs=[SMEM] + [VMEM] * 3 + [ANY] * 16,
        out_specs=[VMEM] * 5,
        scratch_shapes=[pltpu.VMEM((6 * ROWS, HEAD), jnp.float32)] * 3
        + [pltpu.SemaphoreType.DMA((2, GROUPS))],
        compiler_params=pltpu.CompilerParams(vmem_limit_bytes=24 << 20),
        cost_estimate=pl.CostEstimate(flops=1 << 31, bytes_accessed=1 << 22, transcendentals=1 << 22),
        name="attend_others",
    )(info, *qs, *ks, *vs)


def attend_own(info, q, keys, values):
    return pl.pallas_call(
        functools.partial(attend_kernel, 1),
        out_shape=PART,
        in_specs=[SMEM] + [VMEM] * 3,
        out_specs=VMEM,
        scratch_shapes=[pltpu.VMEM((2 * ROWS, HEAD), jnp.float32)] * 3,
        compiler_params=pltpu.CompilerParams(vmem_limit_bytes=4 << 20),
        cost_estimate=pl.CostEstimate(flops=1 << 30, bytes_accessed=1 << 22, transcendentals=1 << 21),
        name="attend_own",
    )(info, q, keys, values)


def combine_kernel(*refs):
    parts, out_ref = refs[:4], refs[4]
    stat = lax.broadcasted_iota(jnp.int32, (STATS, 2 * HEAD), 0)
    head = lax.broadcasted_iota(jnp.int32, (STATS, 2 * HEAD), 1) // HEAD
    is_top = (stat % 4 == 2 * head) & (stat < 12)
    is_total = (stat % 4 == 2 * head + 1) & (stat < 12)

    def spread(ref, which):
        return lax.dot_general(
            ref[ROWS:, :],
            which.astype(jnp.bfloat16),
            (((0,), (0,)), ((), ())),
            preferred_element_type=jnp.float32,
        )

    tops = [spread(ref, is_top) for ref in parts]
    totals = [spread(ref, is_total) for ref in parts]
    best = functools.reduce(jnp.maximum, tops)
    weights = [jnp.exp2((t - best) * SCALE) * n for t, n in zip(tops, totals)]
    numer = sum(w * ref[:ROWS, :].astype(jnp.float32) for w, ref in zip(weights, parts))
    out_ref[...] = (numer / sum(weights)).astype(jnp.bfloat16)


def combine(parts):
    return pl.pallas_call(
        combine_kernel,
        out_shape=jax.ShapeDtypeStruct((ROWS, 2 * HEAD), jnp.bfloat16),
        in_specs=[VMEM] * 4,
        out_specs=VMEM,
        compiler_params=pltpu.CompilerParams(vmem_limit_bytes=4 << 20),
        name="combine",
    )(*parts)


def local(queries, keys, values, offset):
    pb, ka = lax.axis_index("pb"), lax.axis_index("ka")
    x, c, y = pb // 2, pb % 2, ka % 4
    around = (1, 3, 2)

    q1 = send(queries, shift(dy=1))
    key = send(keys, TO_HEAD)
    values, q1 = lax.optimization_barrier((values, q1))
    value = send(values, TO_HEAD)
    q3, q2 = send(queries, shift(dy=3)), send(queries, shift(dy=2))
    key, *qs = lax.optimization_barrier((key, q1, q3, q2))
    k1, k3 = send(key, shift(dx=1)), send(key, shift(dx=3))
    v3, v1 = send(value, shift(dx=3)), send(value, shift(dx=1))
    near_k = [key, k1, k3, send(k1, shift(dx=1))]
    near_v = [value, v1, v3, send(v3, shift(dx=3))]
    far_k = [send(a, shift(dc=1)) for a in near_k]
    far_v = [send(a, shift(dc=1)) for a in near_v]

    slots = [(x - d) % 4 + 4 * c for d in (0,) + around]
    slots += [(x - d) % 4 + 4 * (1 - c) for d in (0,) + around]
    place = offset[0] + pb * (ROWS // BLOCK)
    first = 8 * y
    n_full = jnp.clip((place - first - 7) // 32 + 1, 0, GROUPS)
    n_seen = jnp.clip((place + 3 - first) // 32 + 1, 0, GROUPS)
    info = jnp.stack(slots + [first, place, n_full, n_seen]).astype(jnp.int32)
    *parts, sorted_k, sorted_v = attend_others(info, qs, near_k + far_k, near_v + far_v)
    own = attend_own(info, queries, sorted_k, sorted_v)
    return combine([own] + [send(p, shift(dy=-d)) for p, d in zip(parts, around)])


def solution(mesh):
    placed = (P("pb", "ka"), P("ka", "pb"), P("ka", "pb"), P())
    return jax.shard_map(
        local, mesh=mesh, in_specs=placed, out_specs=P("pb", "ka"), check_vma=False
    )
```

```python
import functools
import math

import jax
import jax.numpy as jnp
from jax import lax
from jax.experimental import pallas as pl
from jax.experimental.pallas import tpu as pltpu
from jax.sharding import PartitionSpec as P

HEAD = 128
BLOCK = 64
CHUNK = 512
GROUPS = 8
ROWS = 256
STATS = 16
NEGATIVE_LARGE = -1e30
UNSEEN = -1e29
SCALE = HEAD ** (-0.5) * math.log2(math.e)
AXES = ("pb", "ka")


def device(x, c, z, y):
    return (x * 2 + c) * 32 + z * 4 + y


PLACES = [
    (x, c, z, y) for x in range(4) for c in range(2) for z in range(8) for y in range(4)
]


def moves(to):
    return [(device(*place), device(*to(*place))) for place in PLACES]


def shift(dx=0, dc=0, dy=0):
    return moves(lambda x, c, z, y: ((x + dx) % 4, (c + dc) % 2, z, (y + dy) % 4))


TO_HEAD = moves(lambda x, c, z, y: (z % 4, z // 4, 2 * x + c, y))


def send(array, pairs):
    return lax.ppermute(array, AXES, pairs)


def attend_kernel(tiles, info, *refs):
    q_refs, keys, values, refs = refs[:tiles], refs[tiles], refs[tiles + 1], refs[tiles + 2 :]
    out_refs, (tops, totals, acc) = refs[:tiles], refs[tiles:]
    first = info[8]
    place = info[9]
    n_full = info[10]
    n_seen = info[11]
    tops[...] = jnp.full(tops.shape, UNSEEN, jnp.float32)
    totals[...] = jnp.zeros_like(totals)
    acc[...] = jnp.zeros_like(acc)

    def step(j, masked):
        key, value = keys[info[j]], values[info[j]]

        def scores(i):
            q = jnp.concatenate([q_refs[i][:, :HEAD], q_refs[i][:, HEAD:]], axis=0)
            s = lax.dot_general(
                q,
                key,
                (((1,), (1,)), ((), ())),
                preferred_element_type=jnp.float32,
            )
            if masked:
                row = lax.broadcasted_iota(jnp.int32, s.shape, 0)
                col = lax.broadcasted_iota(jnp.int32, s.shape, 1)
                seen = first + j * 32 + col // BLOCK <= place + (row % ROWS) // BLOCK
                s = jnp.where(seen, s, NEGATIVE_LARGE)
            return s

        def weights(i, s):
            rows = pl.ds(i * 2 * ROWS, 2 * ROWS)
            old = tops[rows, :]
            top = jnp.maximum(old, jnp.max(s, axis=1, keepdims=True))
            keep = jnp.exp2((old - top) * SCALE)
            p = jnp.exp2((s - jnp.concatenate([top] * 4, axis=1)) * SCALE)
            tops[rows, :] = top
            total = sum(p[:, n * HEAD : (n + 1) * HEAD] for n in range(4))
            totals[rows, :] = totals[rows, :] * keep + total
            return p.astype(jnp.bfloat16), keep

        def mix(i, p, keep):
            rows = pl.ds(i * 2 * ROWS, 2 * ROWS)
            mixed = jnp.dot(p, value, preferred_element_type=jnp.float32)
            acc[rows, :] = acc[rows, :] * keep + mixed

        s, before = scores(0), None
        for i in range(tiles):
            after = scores(i + 1) if i + 1 < tiles else None
            now = weights(i, s)
            if before is not None:
                mix(i - 1, *before)
            before, s = now, after
        mix(tiles - 1, *before)

    def full_step(j, carry):
        step(j, False)
        return carry

    lax.fori_loop(0, n_full, full_step, 0)

    @pl.when(n_seen > n_full)
    def _():
        step(n_full, True)

    lane = lax.broadcasted_iota(jnp.int32, (ROWS, HEAD), 1) % 4
    piece = lax.broadcasted_iota(jnp.int32, (STATS, ROWS), 0) // 4
    for i in range(tiles):
        stats = []
        for h in range(2):
            rows = pl.ds((2 * i + h) * ROWS, ROWS)
            total = jnp.sum(totals[rows, :], axis=1, keepdims=True)
            part = acc[rows, :] / jnp.maximum(total, 1.0)
            out_refs[i][:ROWS, h * HEAD : (h + 1) * HEAD] = part.astype(jnp.bfloat16)
            stats += [tops[rows, :], total]
        packed = jnp.where(
            lane < 2,
            jnp.where(lane == 0, stats[0], stats[1]),
            jnp.where(lane == 2, stats[2], stats[3]),
        )
        rest = packed.T[:STATS, :]
        high = rest.astype(jnp.bfloat16).astype(jnp.float32)
        rest = rest - high
        middle = rest.astype(jnp.bfloat16).astype(jnp.float32)
        low = jnp.where(piece == 2, rest - middle, 0.0)
        pieces = jnp.where(piece == 0, high, jnp.where(piece == 1, middle, low))
        out_refs[i][ROWS:, :] = pieces.astype(jnp.bfloat16)


VMEM = pl.BlockSpec(memory_space=pltpu.VMEM)
SMEM = pl.BlockSpec(memory_space=pltpu.SMEM)
PART = jax.ShapeDtypeStruct((ROWS + STATS, 2 * HEAD), jnp.bfloat16)


def attend(info, qs, keys, values):
    tiles = len(qs)
    return pl.pallas_call(
        functools.partial(attend_kernel, tiles),
        out_shape=[PART] * tiles,
        in_specs=[SMEM] + [VMEM] * (tiles + 2),
        out_specs=[VMEM] * tiles,
        scratch_shapes=[pltpu.VMEM((2 * tiles * ROWS, HEAD), jnp.float32)] * 3,
        compiler_params=pltpu.CompilerParams(vmem_limit_bytes=20 << 20),
        cost_estimate=pl.CostEstimate(
            flops=tiles << 30, bytes_accessed=1 << 22, transcendentals=tiles << 20
        ),
        name=f"attend_{tiles}",
    )(info, *qs, keys, values)


def combine_kernel(*refs):
    parts, out_ref = refs[:4], refs[4]
    stat = lax.broadcasted_iota(jnp.int32, (STATS, 2 * HEAD), 0)
    head = lax.broadcasted_iota(jnp.int32, (STATS, 2 * HEAD), 1) // HEAD
    is_top = (stat % 4 == 2 * head) & (stat < 12)
    is_total = (stat % 4 == 2 * head + 1) & (stat < 12)

    def spread(ref, which):
        return lax.dot_general(
            ref[ROWS:, :],
            which.astype(jnp.bfloat16),
            (((0,), (0,)), ((), ())),
            preferred_element_type=jnp.float32,
        )

    tops = [spread(ref, is_top) for ref in parts]
    totals = [spread(ref, is_total) for ref in parts]
    best = functools.reduce(jnp.maximum, tops)
    weights = [jnp.exp2((t - best) * SCALE) * n for t, n in zip(tops, totals)]
    numer = sum(w * ref[:ROWS, :].astype(jnp.float32) for w, ref in zip(weights, parts))
    out_ref[...] = (numer / sum(weights)).astype(jnp.bfloat16)


def combine(parts):
    return pl.pallas_call(
        combine_kernel,
        out_shape=jax.ShapeDtypeStruct((ROWS, 2 * HEAD), jnp.bfloat16),
        in_specs=[VMEM] * 4,
        out_specs=VMEM,
        compiler_params=pltpu.CompilerParams(vmem_limit_bytes=4 << 20),
        name="combine",
    )(*parts)


def local(queries, keys, values, offset):
    pb, ka = lax.axis_index("pb"), lax.axis_index("ka")
    x, c, y = pb // 2, pb % 2, ka % 4
    around = (1, 3, 2)

    q1 = send(queries, shift(dy=1))
    key = send(keys, TO_HEAD)
    values, q1 = lax.optimization_barrier((values, q1))
    value = send(values, TO_HEAD)
    q3, q2 = send(queries, shift(dy=3)), send(queries, shift(dy=2))
    key, *qs = lax.optimization_barrier((key, q1, q3, q2))
    k1, k3 = send(key, shift(dx=1)), send(key, shift(dx=3))
    v3, v1 = send(value, shift(dx=3)), send(value, shift(dx=1))
    near_k = [key, k1, k3, send(k1, shift(dx=1))]
    near_v = [value, v1, v3, send(v3, shift(dx=3))]
    far_k = [send(a, shift(dc=1)) for a in near_k]
    far_v = [send(a, shift(dc=1)) for a in near_v]

    order = jnp.array([0, 1, 3, 2], jnp.int32)[(x - jnp.arange(4)) % 4]
    slots = jnp.concatenate([order + 4 * c, order + 4 * (1 - c)])
    place = offset[0] + pb * (ROWS // BLOCK)
    first = 8 * y
    n_full = jnp.clip((place - first - 7) // 32 + 1, 0, GROUPS)
    n_seen = jnp.clip((place + 3 - first) // 32 + 1, 0, GROUPS)
    limits = jnp.stack([first, place, n_full, n_seen]).astype(jnp.int32)
    info = jnp.concatenate([slots.astype(jnp.int32), limits])
    kv = lax.optimization_barrier(near_k + far_k + near_v + far_v)
    keys = jnp.concatenate(kv[:GROUPS]).reshape(GROUPS, CHUNK, HEAD)
    values = jnp.concatenate(kv[GROUPS:]).reshape(GROUPS, CHUNK, HEAD)
    parts = attend(info, qs, keys, values)
    (own,) = attend(info, [queries], keys, values)
    return combine([own] + [send(p, shift(dy=-d)) for p, d in zip(parts, around)])


def solution(mesh):
    placed = (P("pb", "ka"), P("ka", "pb"), P("ka", "pb"), P())
    return jax.shard_map(
        local, mesh=mesh, in_specs=placed, out_specs=P("pb", "ka"), check_vma=False
    )
```

```python
import functools
import math

import jax
import jax.numpy as jnp
from jax import lax
from jax.experimental import pallas as pl
from jax.experimental.pallas import tpu as pltpu
from jax.sharding import PartitionSpec as P

HEAD = 128
BLOCK = 64
CHUNK = 512
GROUPS = 8
ROWS = 256
STATS = 16
NEGATIVE_LARGE = -1e30
UNSEEN = -1e29
SCALE = HEAD ** (-0.5) * math.log2(math.e)
AXES = ("pb", "ka")


def device(x, c, z, y):
    return (x * 2 + c) * 32 + z * 4 + y


PLACES = [
    (x, c, z, y) for x in range(4) for c in range(2) for z in range(8) for y in range(4)
]


def moves(to):
    return [(device(*place), device(*to(*place))) for place in PLACES]


def shift(dx=0, dc=0, dy=0):
    return moves(lambda x, c, z, y: ((x + dx) % 4, (c + dc) % 2, z, (y + dy) % 4))


TO_HEAD = moves(lambda x, c, z, y: (z % 4, z // 4, 2 * x + c, y))


def send(array, pairs):
    return lax.ppermute(array, AXES, pairs)


def attend_kernel(tiles, info, *refs):
    q_refs, keys, values, refs = refs[:tiles], refs[tiles], refs[tiles + 1], refs[tiles + 2 :]
    out_refs, (tops, totals, acc) = refs[:tiles], refs[tiles:]
    first = info[8]
    place = info[9]
    n_full = info[10]
    n_seen = info[11]
    tops[...] = jnp.full(tops.shape, UNSEEN, jnp.float32)
    totals[...] = jnp.zeros_like(totals)
    acc[...] = jnp.zeros_like(acc)

    def step(j, masked):
        key, value = keys[info[j]], values[info[j]]

        def scores(i):
            q = jnp.concatenate([q_refs[i][:, :HEAD], q_refs[i][:, HEAD:]], axis=0)
            s = lax.dot_general(
                q,
                key,
                (((1,), (1,)), ((), ())),
                preferred_element_type=jnp.float32,
            )
            if masked:
                row = lax.broadcasted_iota(jnp.int32, s.shape, 0)
                col = lax.broadcasted_iota(jnp.int32, s.shape, 1)
                seen = first + j * 32 + col // BLOCK <= place + (row % ROWS) // BLOCK
                s = jnp.where(seen, s, NEGATIVE_LARGE)
            return s

        def weights(i, s):
            rows = pl.ds(i * 2 * ROWS, 2 * ROWS)
            old = tops[rows, :]
            top = jnp.maximum(old, jnp.max(s, axis=1, keepdims=True))
            keep = jnp.exp2((old - top) * SCALE)
            p = jnp.exp2((s - jnp.concatenate([top] * 4, axis=1)) * SCALE)
            tops[rows, :] = top
            total = sum(p[:, n * HEAD : (n + 1) * HEAD] for n in range(4))
            totals[rows, :] = totals[rows, :] * keep + total
            return p.astype(jnp.bfloat16), keep

        def mix(i, p, keep):
            rows = pl.ds(i * 2 * ROWS, 2 * ROWS)
            mixed = jnp.dot(p, value, preferred_element_type=jnp.float32)
            acc[rows, :] = acc[rows, :] * keep + mixed

        s, before = scores(0), None
        for i in range(tiles):
            after = scores(i + 1) if i + 1 < tiles else None
            now = weights(i, s)
            if before is not None:
                mix(i - 1, *before)
            before, s = now, after
        mix(tiles - 1, *before)

    def full_step(j, carry):
        step(j, False)
        return carry

    lax.fori_loop(0, n_full, full_step, 0)

    @pl.when(n_seen > n_full)
    def _():
        step(n_full, True)

    lane = lax.broadcasted_iota(jnp.int32, (ROWS, HEAD), 1) % 4
    piece = lax.broadcasted_iota(jnp.int32, (STATS, ROWS), 0) // 4
    for i in range(tiles):
        stats = []
        for h in range(2):
            rows = pl.ds((2 * i + h) * ROWS, ROWS)
            total = jnp.sum(totals[rows, :], axis=1, keepdims=True)
            part = acc[rows, :] / jnp.maximum(total, 1.0)
            out_refs[i][:ROWS, h * HEAD : (h + 1) * HEAD] = part.astype(jnp.bfloat16)
            stats += [tops[rows, :], total]
        packed = jnp.where(
            lane < 2,
            jnp.where(lane == 0, stats[0], stats[1]),
            jnp.where(lane == 2, stats[2], stats[3]),
        )
        rest = packed.T[:STATS, :]
        high = rest.astype(jnp.bfloat16).astype(jnp.float32)
        rest = rest - high
        middle = rest.astype(jnp.bfloat16).astype(jnp.float32)
        low = jnp.where(piece == 2, rest - middle, 0.0)
        pieces = jnp.where(piece == 0, high, jnp.where(piece == 1, middle, low))
        out_refs[i][ROWS:, :] = pieces.astype(jnp.bfloat16)


VMEM = pl.BlockSpec(memory_space=pltpu.VMEM)
SMEM = pl.BlockSpec(memory_space=pltpu.SMEM)
PART = jax.ShapeDtypeStruct((ROWS + STATS, 2 * HEAD), jnp.bfloat16)


def attend(info, qs, keys, values):
    tiles = len(qs)
    return pl.pallas_call(
        functools.partial(attend_kernel, tiles),
        out_shape=[PART] * tiles,
        in_specs=[SMEM] + [VMEM] * (tiles + 2),
        out_specs=[VMEM] * tiles,
        scratch_shapes=[pltpu.VMEM((2 * tiles * ROWS, HEAD), jnp.float32)] * 3,
        compiler_params=pltpu.CompilerParams(vmem_limit_bytes=20 << 20),
        cost_estimate=pl.CostEstimate(
            flops=tiles << 30, bytes_accessed=1 << 22, transcendentals=tiles << 20
        ),
        name=f"attend_{tiles}",
    )(info, *qs, keys, values)


def combine_kernel(*refs):
    parts, out_ref = refs[:4], refs[4]
    stat = lax.broadcasted_iota(jnp.int32, (STATS, 2 * HEAD), 0)
    head = lax.broadcasted_iota(jnp.int32, (STATS, 2 * HEAD), 1) // HEAD
    is_top = (stat % 4 == 2 * head) & (stat < 12)
    is_total = (stat % 4 == 2 * head + 1) & (stat < 12)

    def spread(ref, which):
        return lax.dot_general(
            ref[ROWS:, :],
            which.astype(jnp.bfloat16),
            (((0,), (0,)), ((), ())),
            preferred_element_type=jnp.float32,
        )

    tops = [spread(ref, is_top) for ref in parts]
    totals = [spread(ref, is_total) for ref in parts]
    best = functools.reduce(jnp.maximum, tops)
    weights = [jnp.exp2((t - best) * SCALE) * n for t, n in zip(tops, totals)]
    numer = sum(w * ref[:ROWS, :].astype(jnp.float32) for w, ref in zip(weights, parts))
    out_ref[...] = (numer / sum(weights)).astype(jnp.bfloat16)


def combine(parts):
    return pl.pallas_call(
        combine_kernel,
        out_shape=jax.ShapeDtypeStruct((ROWS, 2 * HEAD), jnp.bfloat16),
        in_specs=[VMEM] * 4,
        out_specs=VMEM,
        compiler_params=pltpu.CompilerParams(vmem_limit_bytes=4 << 20),
        name="combine",
    )(*parts)


def local(queries, keys, values, offset):
    pb, ka = lax.axis_index("pb"), lax.axis_index("ka")
    x, c, y = pb // 2, pb % 2, ka % 4
    around = (1, 3, 2)

    key = send(keys, TO_HEAD)
    q1 = send(queries, shift(dy=1))
    value = send(values, TO_HEAD)
    q3, q2 = send(queries, shift(dy=3)), send(queries, shift(dy=2))
    key, *qs = lax.optimization_barrier((key, q1, q3, q2))

    def gather(own):
        n2, n1, n3 = [send(own, shift(dx=d)) for d in (2, 1, 3)]
        return lax.optimization_barrier(jnp.concatenate([own, n1, n3, n2]))

    near_k, near_v = gather(key), gather(value)
    far_k, far_v = send(near_k, shift(dc=1)), send(near_v, shift(dc=1))

    order = jnp.array([0, 1, 3, 2], jnp.int32)[(x - jnp.arange(4)) % 4]
    slots = jnp.concatenate([order + 4 * c, order + 4 * (1 - c)])
    place = offset[0] + pb * (ROWS // BLOCK)
    first = 8 * y
    n_full = jnp.clip((place - first - 7) // 32 + 1, 0, GROUPS)
    n_seen = jnp.clip((place + 3 - first) // 32 + 1, 0, GROUPS)
    limits = jnp.stack([first, place, n_full, n_seen]).astype(jnp.int32)
    info = jnp.concatenate([slots.astype(jnp.int32), limits])
    near_k, far_k, near_v, far_v = lax.optimization_barrier((near_k, far_k, near_v, far_v))
    keys = jnp.concatenate([near_k, far_k]).reshape(GROUPS, CHUNK, HEAD)
    values = jnp.concatenate([near_v, far_v]).reshape(GROUPS, CHUNK, HEAD)
    parts = attend(info, qs, keys, values)
    (own,) = attend(info, [queries], keys, values)
    next_part, previous_part, far_part = parts
    far_part = send(far_part, shift(dy=2))
    next_part, previous_part = send(next_part, shift(dy=-1)), send(previous_part, shift(dy=1))
    return combine([own, next_part, previous_part, far_part])


def solution(mesh):
    placed = (P("pb", "ka"), P("ka", "pb"), P("ka", "pb"), P())
    return jax.shard_map(
        local, mesh=mesh, in_specs=placed, out_specs=P("pb", "ka"), check_vma=False
    )
```

```python
import functools
import math

import jax
import jax.numpy as jnp
from jax import lax
from jax.experimental import pallas as pl
from jax.experimental.pallas import tpu as pltpu
from jax.sharding import PartitionSpec as P

HEAD = 128
BLOCK = 64
CHUNK = 512
GROUPS = 8
ROWS = 256
STATS = 16
NEGATIVE_LARGE = -1e30
UNSEEN = -1e29
SCALE = HEAD ** (-0.5) * math.log2(math.e)
AXES = ("pb", "ka")


def device(x, c, z, y):
    return (x * 2 + c) * 32 + z * 4 + y


PLACES = [
    (x, c, z, y) for x in range(4) for c in range(2) for z in range(8) for y in range(4)
]


def moves(to):
    return [(device(*place), device(*to(*place))) for place in PLACES]


def shift(dx=0, dc=0, dy=0):
    return moves(lambda x, c, z, y: ((x + dx) % 4, (c + dc) % 2, z, (y + dy) % 4))


TO_HEAD = moves(lambda x, c, z, y: (z % 4, z // 4, 2 * x + c, y))


def send(array, pairs):
    return lax.ppermute(array, AXES, pairs)


def attend_kernel(tiles, info, *refs):
    q_refs, keys, values, refs = refs[:tiles], refs[tiles], refs[tiles + 1], refs[tiles + 2 :]
    out_refs, (tops, totals, acc) = refs[:tiles], refs[tiles:]
    first = info[8]
    place = info[9]
    n_full = info[10]
    n_seen = info[11]
    tops[...] = jnp.full(tops.shape, UNSEEN, jnp.float32)
    totals[...] = jnp.zeros_like(totals)
    acc[...] = jnp.zeros_like(acc)

    def step(slots, masked):
        at = [info[j] for j in slots]
        key, value = [keys[j] for j in at], [values[j] for j in at]

        def scores(i):
            q = jnp.concatenate([q_refs[i][:, :HEAD], q_refs[i][:, HEAD:]], axis=0)
            s = [
                lax.dot_general(
                    q,
                    some,
                    (((1,), (1,)), ((), ())),
                    preferred_element_type=jnp.float32,
                )
                for some in key
            ]
            s = jnp.concatenate(s, axis=1) if len(s) > 1 else s[0]
            if masked:
                row = lax.broadcasted_iota(jnp.int32, s.shape, 0)
                col = lax.broadcasted_iota(jnp.int32, s.shape, 1)
                seen = first + slots[0] * 32 + col // BLOCK <= place + (row % ROWS) // BLOCK
                s = jnp.where(seen, s, NEGATIVE_LARGE)
            return s

        def weights(i, s):
            rows = pl.ds(i * 2 * ROWS, 2 * ROWS)
            old = tops[rows, :]
            top = jnp.maximum(old, jnp.max(s, axis=1, keepdims=True))
            keep = jnp.exp2((old - top) * SCALE)
            p = jnp.exp2((s - jnp.concatenate([top] * (s.shape[1] // HEAD), axis=1)) * SCALE)
            tops[rows, :] = top
            total = sum(p[:, n : n + HEAD] for n in range(0, s.shape[1], HEAD))
            totals[rows, :] = totals[rows, :] * keep + total
            return p.astype(jnp.bfloat16), keep

        def mix(i, p, keep):
            rows = pl.ds(i * 2 * ROWS, 2 * ROWS)
            mixed = sum(
                jnp.dot(
                    p[:, n * CHUNK : (n + 1) * CHUNK],
                    some,
                    preferred_element_type=jnp.float32,
                )
                for n, some in enumerate(value)
            )
            acc[rows, :] = acc[rows, :] * keep + mixed

        s, before = scores(0), None
        for i in range(tiles):
            after = scores(i + 1) if i + 1 < tiles else None
            now = weights(i, s)
            if before is not None:
                mix(i - 1, *before)
            before, s = now, after
        mix(tiles - 1, *before)

    def full_steps(j, carry):
        step([2 * j, 2 * j + 1], False)
        return carry

    def masked_step(j, carry):
        step([j], True)
        return carry

    lax.fori_loop(0, n_full // 2, full_steps, 0)
    lax.fori_loop(n_full // 2 * 2, n_seen, masked_step, 0)

    lane = lax.broadcasted_iota(jnp.int32, (ROWS, HEAD), 1) % 4
    piece = lax.broadcasted_iota(jnp.int32, (STATS, ROWS), 0) // 4
    for i in range(tiles):
        stats = []
        for h in range(2):
            rows = pl.ds((2 * i + h) * ROWS, ROWS)
            total = jnp.sum(totals[rows, :], axis=1, keepdims=True)
            part = acc[rows, :] / jnp.maximum(total, 1.0)
            out_refs[i][:ROWS, h * HEAD : (h + 1) * HEAD] = part.astype(jnp.bfloat16)
            stats += [tops[rows, :], total]
        packed = jnp.where(
            lane < 2,
            jnp.where(lane == 0, stats[0], stats[1]),
            jnp.where(lane == 2, stats[2], stats[3]),
        )
        rest = packed.T[:STATS, :]
        high = rest.astype(jnp.bfloat16).astype(jnp.float32)
        rest = rest - high
        middle = rest.astype(jnp.bfloat16).astype(jnp.float32)
        low = jnp.where(piece == 2, rest - middle, 0.0)
        pieces = jnp.where(piece == 0, high, jnp.where(piece == 1, middle, low))
        out_refs[i][ROWS:, :] = pieces.astype(jnp.bfloat16)


VMEM = pl.BlockSpec(memory_space=pltpu.VMEM)
SMEM = pl.BlockSpec(memory_space=pltpu.SMEM)
PART = jax.ShapeDtypeStruct((ROWS + STATS, 2 * HEAD), jnp.bfloat16)


def attend(info, qs, keys, values):
    tiles = len(qs)
    return pl.pallas_call(
        functools.partial(attend_kernel, tiles),
        out_shape=[PART] * tiles,
        in_specs=[SMEM] + [VMEM] * (tiles + 2),
        out_specs=[VMEM] * tiles,
        scratch_shapes=[pltpu.VMEM((2 * tiles * ROWS, HEAD), jnp.float32)] * 3,
        compiler_params=pltpu.CompilerParams(vmem_limit_bytes=20 << 20),
        cost_estimate=pl.CostEstimate(
            flops=tiles << 30, bytes_accessed=1 << 22, transcendentals=tiles << 20
        ),
        name=f"attend_{tiles}",
    )(info, *qs, keys, values)


def combine_kernel(*refs):
    parts, out_ref = refs[:4], refs[4]
    stat = lax.broadcasted_iota(jnp.int32, (STATS, 2 * HEAD), 0)
    head = lax.broadcasted_iota(jnp.int32, (STATS, 2 * HEAD), 1) // HEAD
    is_top = (stat % 4 == 2 * head) & (stat < 12)
    is_total = (stat % 4 == 2 * head + 1) & (stat < 12)

    def spread(ref, which):
        return lax.dot_general(
            ref[ROWS:, :],
            which.astype(jnp.bfloat16),
            (((0,), (0,)), ((), ())),
            preferred_element_type=jnp.float32,
        )

    tops = [spread(ref, is_top) for ref in parts]
    totals = [spread(ref, is_total) for ref in parts]
    best = functools.reduce(jnp.maximum, tops)
    weights = [jnp.exp2((t - best) * SCALE) * n for t, n in zip(tops, totals)]
    numer = sum(w * ref[:ROWS, :].astype(jnp.float32) for w, ref in zip(weights, parts))
    out_ref[...] = (numer / sum(weights)).astype(jnp.bfloat16)


def combine(parts):
    return pl.pallas_call(
        combine_kernel,
        out_shape=jax.ShapeDtypeStruct((ROWS, 2 * HEAD), jnp.bfloat16),
        in_specs=[VMEM] * 4,
        out_specs=VMEM,
        compiler_params=pltpu.CompilerParams(vmem_limit_bytes=4 << 20),
        name="combine",
    )(*parts)


def local(queries, keys, values, offset):
    pb, ka = lax.axis_index("pb"), lax.axis_index("ka")
    x, c, y = pb // 2, pb % 2, ka % 4
    around = (1, 3, 2)

    key = send(keys, TO_HEAD)
    q1 = send(queries, shift(dy=1))
    value = send(values, TO_HEAD)
    q3, q2 = send(queries, shift(dy=3)), send(queries, shift(dy=2))
    key, *qs = lax.optimization_barrier((key, q1, q3, q2))
    k2, k1, k3 = [send(key, shift(dx=d)) for d in (2, 1, 3)]
    near_k = [key, k1, k3, k2]
    v2, v1, v3 = [send(value, shift(dx=d)) for d in (2, 1, 3)]
    near_v = [value, v1, v3, v2]

    near_k = [lax.optimization_barrier(jnp.concatenate(near_k))]
    far_k = [send(a, shift(dc=1)) for a in near_k]
    near_v = [lax.optimization_barrier(jnp.concatenate(near_v))]
    far_v = [send(a, shift(dc=1)) for a in near_v]

    order = jnp.array([0, 1, 3, 2], jnp.int32)[(x - jnp.arange(4)) % 4]
    slots = jnp.concatenate([order + 4 * c, order + 4 * (1 - c)])
    place = offset[0] + pb * (ROWS // BLOCK)
    first = 8 * y
    n_full = jnp.clip((place - first - 7) // 32 + 1, 0, GROUPS)
    n_seen = jnp.clip((place + 3 - first) // 32 + 1, 0, GROUPS)
    limits = jnp.stack([first, place, n_full, n_seen]).astype(jnp.int32)
    info = jnp.concatenate([slots.astype(jnp.int32), limits])
    kv = lax.optimization_barrier(near_k + far_k + near_v + far_v)
    n = len(near_k + far_k)
    keys = jnp.concatenate(kv[:n]).reshape(GROUPS, CHUNK, HEAD)
    values = jnp.concatenate(kv[n:]).reshape(GROUPS, CHUNK, HEAD)
    parts = attend(info, qs, keys, values)
    (own,) = attend(info, [queries], keys, values)
    next_part, previous_part, far_part = parts
    far_part = send(far_part, shift(dy=2))
    next_part, previous_part = send(next_part, shift(dy=-1)), send(previous_part, shift(dy=1))
    return combine([own, next_part, previous_part, far_part])


def solution(mesh):
    placed = (P("pb", "ka"), P("ka", "pb"), P("ka", "pb"), P())
    return jax.shard_map(
        local, mesh=mesh, in_specs=placed, out_specs=P("pb", "ka"), check_vma=False
    )
```
